32 devices in a mesh: storm: 2 (over x), dom: 16 (over z, y, core).
Axes of the slice: x: 2, y: 2, z: 4, core: 2. Of those that a mesh axis runs over, the one named last changes fastest.
Arguments:
- eta_start: float32 [2048, 128], P(('storm', 'dom')), parts along dimension 0, may hold values from -4 to 4
- forcing: float32 [4, 2048, 128], P(None, ('storm', 'dom')), parts along dimension 1, may hold values from -3 to 3
- diagonal: float32 [1024, 128], P('dom'), may hold values from 1 to 2
- coupling: bfloat16 [1024, 4, 128, 128], P('dom'), may hold values from -0.5 to 0.5
- neighbours: int32 [1024, 4], P('dom'), may hold values from 0 to 127, as said below
- wet: int32 [1024, 128], P('dom'), may hold values 0 or 1
- grid_nodes: int32 [3, 131072], P(None, 'dom'), may hold values from 0 to 8191
- grid_weights: float32 [3, 131072], P(None, 'dom'), may hold values from 0 to 1, as said below
Outputs:
- return_level: float32 [262144], P(('storm', 'dom')), parts along dimension 0
- grid_final: float32 [262144], P(('storm', 'dom')), parts along dimension 0
The draws below stay inside these ranges and needn't reach their ends.
There are 2 independent parts, one for each index of `storm`. The reference program is written for one: setup_inputs(seed, part) draws one part's arguments, and reference() takes and returns one part's arrays. A program takes and returns all parts, laid end to end along the dimension named above; an argument that names none is the same for every part. Nothing has to cross between parts.
Inputs may be any that keep to these rules, and one draw needn't show every extreme that they name: `neighbours`: entries index the 32 blocks before a partition's own 64, those, and the 32 after, counted from 0; slot 0 of a row is the row's own block; the slots of a row name distinct blocks. `grid_weights`: Nonnegative; the three weights of a cell sum to one.
All inputs are finite; a program needn't handle non-finite values. No bound on the sum of `wet` on one device may be relied on, other than what follows from the above.
Results may differ from the reference program's by a relative error of at most 0.0003.
Values may be sent and summed in bfloat16 or wider, within the bound.
A program may use at most 64 MiB of HBM per device.

```python
import math
import jax
import jax.numpy as jnp
from jax import lax

PARTITION_BLOCKS = 64
NODE = 128
SLOTS = 4
STEPS = 4
SWEEPS = 8
BLOCKS = 1024
GRID = 131072
N_DOM = 16


def draw_neighbours(key, part):
    key = jax.random.fold_in(key, 11)
    margin_rows = PARTITION_BLOCKS // 2
    option_count = 2 * margin_rows
    offsets = jnp.concatenate([jnp.arange(-margin_rows, 0, dtype=jnp.int32), jnp.arange(1, margin_rows + 1, dtype=jnp.int32)])
    candidate_option = jnp.arange(option_count, dtype=jnp.int32)[None, :]
    ranking_values = jax.random.randint(key, (BLOCKS, option_count), 0, 1 << 20) * option_count + candidate_option
    partition_row = (jnp.arange(BLOCKS, dtype=jnp.int32) % PARTITION_BLOCKS)[:, None]
    leading_reward = jnp.where((partition_row == 0) & (candidate_option == 0), 1 << 27, 0)
    trailing_reward = jnp.where((partition_row == PARTITION_BLOCKS - 1) & (candidate_option == option_count - 1), 1 << 27, 0)
    ranking_values = ranking_values + leading_reward + trailing_reward
    picked = lax.top_k(ranking_values, SLOTS - 1)[1]
    others = margin_rows + partition_row + offsets[picked]
    itself = margin_rows + partition_row
    return jnp.concatenate([itself, others], axis=1).astype(jnp.int32)


def draw_grid_weights(key, part):
    key = jax.random.fold_in(key, 5)
    raw_weights = jax.random.uniform(key, (3, GRID), jnp.float32, 0.2, 1.0)
    return raw_weights / jnp.sum(raw_weights, axis=0, keepdims=True)


def with_ends(values, key, smallest, largest):
    extent = values.shape
    spot = [jax.random.randint(jax.random.fold_in(key, axis), (), 0, extent[axis]) for axis in range(len(extent))]
    values = values.at[tuple(spot)].set(smallest)
    longest = extent.index(max(extent))
    spot[longest] = (spot[longest] + 1) % extent[longest]
    return values.at[tuple(spot)].set(largest)


def level_of(own_key, shape, pieces, low, top_value):
    loudness = 1.0
    for axis_at, blocks in pieces:
        heights = jax.random.uniform(jax.random.fold_in(jax.random.fold_in(own_key, 6), axis_at), (blocks,), jnp.float32, low / len(pieces), top_value / len(pieces))
        loudness = loudness * jnp.repeat(jnp.exp(heights), shape[axis_at] // blocks).reshape((-1,) + (1,) * (len(shape) - 1 - axis_at))
    return loudness


def noise(own_key, shape, scale, reach, pieces=(), kind=jnp.bfloat16):
    result = jax.random.normal(own_key, shape, jnp.float32) * scale
    if len(pieces) > 0:
        result = level_of(own_key, shape, pieces, -0.22, 0.18) * result
    return jnp.clip(result, min=-reach, max=reach).astype(kind)


def setup_inputs(seed: int = 0, part: int = 0) -> dict:
    keys = jax.random.split(jax.random.key(seed), 9)
    own_keys = jax.random.split(jax.random.fold_in(keys[8], part), 9)
    return {
        "eta_start": noise(own_keys[0], (BLOCKS, NODE), 0.5, 4.0, ((0, 16),), jnp.float32),
        "forcing": noise(own_keys[1], (STEPS, BLOCKS, NODE), 0.3, 3.0, ((1, 16),), jnp.float32),
        "diagonal": jnp.clip(jnp.exp(math.log(2.0) - 0.6931472 * jax.random.uniform(keys[2], (BLOCKS, NODE), jnp.float32) ** level_of(keys[2], (BLOCKS, NODE), ((0, 16),), -0.2, 0.2)), 1.0, 2.0),
        "coupling": noise(keys[3], (BLOCKS, SLOTS, NODE, NODE), (17 * (400 * SLOTS * NODE) ** -0.5), 0.5, ((0, 16),)),
        "neighbours": draw_neighbours(jax.random.fold_in(keys[8], 71), part),
        "wet": with_ends((jax.random.randint(keys[5], (BLOCKS, NODE), 0, 8) < 7).astype(jnp.int32), jax.random.fold_in(keys[5], 1), 0, 1),
        "grid_nodes": with_ends(jax.random.randint(keys[6], (3, GRID), 0, PARTITION_BLOCKS * NODE), jax.random.fold_in(keys[6], 1), 0, (PARTITION_BLOCKS * NODE) - 1).astype(jnp.int32),
        "grid_weights": draw_grid_weights(jax.random.fold_in(keys[8], 71), part),
    }


def to_grid(values_in, grid_nodes, grid_weights):
    domains = N_DOM
    per_strip = PARTITION_BLOCKS * NODE
    arranged = values_in.reshape(domains, domains, per_strip // domains)
    arranged = jnp.transpose(arranged, (1, 0, 2)).reshape(domains, per_strip)
    indices = grid_nodes.reshape(3, domains, per_strip)
    sampled = jnp.take_along_axis(jnp.broadcast_to(arranged[None], (3, domains, per_strip)), indices, axis=2)
    return jnp.sum(grid_weights.reshape(3, domains, per_strip) * sampled, axis=0).reshape(GRID)


def reference(eta_start, forcing, diagonal, coupling, neighbours, wet, grid_nodes, grid_weights):
    margin_rows = PARTITION_BLOCKS // 2
    block_rows = jnp.arange(BLOCKS, dtype=jnp.int32)
    owner_part = block_rows // PARTITION_BLOCKS
    target = (owner_part * PARTITION_BLOCKS)[:, None] + neighbours.astype(jnp.int32)
    coupling_wide = coupling.astype(jnp.float32)
    wet_share = wet.astype(jnp.float32)
    surface = eta_start
    snapshots = []
    for step_index in range(STEPS):
        source = diagonal * surface + forcing[step_index]
        iterate = surface
        for sweep_index in range(SWEEPS):
            padded = jnp.pad(iterate, ((margin_rows, margin_rows), (0, 0)))
            nearby = padded[target]
            coupled = jnp.einsum("bsij,bsj->bi", coupling_wide, nearby, precision=lax.Precision.HIGHEST)
            iterate = wet_share * (source - coupled) / diagonal
        surface = iterate
        snapshots.append(surface)
    highest = snapshots[0]
    for later in snapshots[1:]:
        highest = jnp.maximum(highest, later)
    latest = snapshots[-1]
    return to_grid(highest, grid_nodes, grid_weights), to_grid(latest, grid_nodes, grid_weights)
```

```python
import functools

import jax
import jax.numpy as jnp
from jax import lax
from jax.experimental import pallas as pl
from jax.experimental.pallas import tpu as pltpu
from jax.sharding import PartitionSpec as P

SWEEPS = 8
MESH = pl.DeviceIdType.MESH
F32, BF16 = jnp.float32, jnp.bfloat16


def surge_kernel(
    domains,
    eta_ref, forcing_ref, diag_ref, nb_ref, wet_ref, coupling_ref,
    out_ref,
    raw, weights, padded, onehot, surface, source, scale, highest, partial, sending, landing,
    load_sem, send_sem, recv_sem, strip_send, strip_recv,
):
    steps, rows, node = forcing_ref.shape
    slots = coupling_ref.shape[1]
    margin = rows // 2
    share = rows // domains
    chunk = 8
    me = lax.axis_index("dom")
    has_left, has_right = me > 0, me < domains - 1

    loads = [
        pltpu.make_async_copy(
            coupling_ref.at[pl.ds(c * chunk, chunk)], raw.at[pl.ds(c * chunk, chunk)], load_sem.at[c]
        )
        for c in range(rows // chunk)
    ]
    for load in loads:
        load.start()

    padded[...] = jnp.zeros_like(padded)
    barrier = pltpu.get_barrier_semaphore()

    def greet(k, carry):
        peer = lax.rem(me + k, domains)
        pl.semaphore_signal(barrier, inc=1, device_id={"dom": peer}, device_id_type=MESH)
        return carry

    lax.fori_loop(1, domains, greet, 0)

    scale[...] = wet_ref[...].astype(F32) / diag_ref[...]
    lane = lax.broadcasted_iota(jnp.int32, (rows, 2 * rows), 1)
    for s in range(1, slots):
        onehot[(s - 1) * rows : s * rows, :] = (nb_ref[:, s : s + 1] == lane).astype(F32).astype(BF16)

    def split(value):
        high = value.astype(BF16).astype(F32)
        return high, value - high

    def store(slot, row, count):
        high, low = split(surface[row : row + count, :])
        padded[slot, margin + row : margin + row + count, :node] = high.astype(BF16)
        padded[slot, margin + row : margin + row + count, node:] = low.astype(BF16)

    def exchange(slot, side):
        return pltpu.make_async_remote_copy(
            src_ref=padded.at[slot, pl.ds(margin + side * margin, margin)],
            dst_ref=padded.at[slot, pl.ds(margin + rows if side == 0 else 0, margin)],
            send_sem=send_sem.at[slot, side],
            recv_sem=recv_sem.at[slot, side],
            device_id={"dom": me - 1 if side == 0 else me + 1},
            device_id_type=MESH,
        )

    def arrival(slot, side):
        return pltpu.make_async_remote_copy(
            src_ref=padded.at[slot, pl.ds(margin + side * margin, margin)],
            dst_ref=padded.at[slot, pl.ds(margin + rows if side == 0 else 0, margin)],
            send_sem=send_sem.at[slot, side],
            recv_sem=recv_sem.at[slot, side],
            device_id={"dom": me + 1 if side == 0 else me - 1},
            device_id_type=MESH,
        )

    def send(slot, side, condition):
        @pl.when(jnp.logical_and(has_left if side == 0 else has_right, condition))
        def _():
            exchange(slot, side).start()

    surface[...] = eta_ref[...]
    source[...] = diag_ref[...] * eta_ref[...] + forcing_ref[0]
    highest[...] = jnp.full((rows, node), -jnp.inf, F32)
    store(0, 0, rows)

    pl.semaphore_wait(barrier, domains - 1)
    send(0, 0, True)
    send(0, 1, True)

    for c, load in enumerate(loads):
        load.wait()

        def arrange(pair, carry):
            for half in range(2):
                for s in range(slots):
                    weights[pair, s * node : (s + 1) * node, half * node : (half + 1) * node] = raw[
                        2 * pair + half, s
                    ].T
            return carry

        lax.fori_loop(c * chunk // 2, (c + 1) * chunk // 2, arrange, 0)

    sub = lax.broadcasted_iota(jnp.int32, (8, node), 0)

    def products(group, left, first, last):
        result = jnp.zeros((8, node), F32)
        for q in range(4):
            pair = group * 4 + q
            both = jnp.dot(
                left, weights[pair, first * node : last * node, :], preferred_element_type=F32
            )
            both = both[:8] + both[8:]
            result = jnp.where(sub == 2 * q, both[:, :node], result)
            result = jnp.where(sub == 2 * q + 1, both[:, node:], result)
        return result

    def sweep(slot, more):
        for group in range(rows // 8):
            at = slice(group * 8, group * 8 + 8)
            left = jnp.concatenate(split(surface[at, :]), axis=0).astype(BF16)
            partial[at, :] = products(group, left, 0, 1)

        @pl.when(has_right)
        def _():
            arrival(slot, 0).wait_recv()
            exchange(slot, 1).wait_send()

        @pl.when(has_left)
        def _():
            arrival(slot, 1).wait_recv()
            exchange(slot, 0).wait_send()

        near = jnp.dot(onehot[...], padded[slot], preferred_element_type=F32)
        for group in range(rows // 8):
            at = slice(group * 8, group * 8 + 8)
            left = jnp.concatenate(
                [
                    jnp.concatenate(
                        [
                            near[s * rows + group * 8 : s * rows + group * 8 + 8, :node],
                            near[s * rows + group * 8 : s * rows + group * 8 + 8, node:],
                        ],
                        axis=0,
                    )
                    for s in range(slots - 1)
                ],
                axis=1,
            ).astype(BF16)
            coupled = partial[at, :] + products(group, left, 1, slots)
            surface[at, :] = (source[at, :] - coupled) * scale[at, :]
            if group % 2 == 1:
                store(1 - slot, group * 8 - 8, 16)
            if group == rows // 16 - 1:
                send(1 - slot, 0, more)
            if group == rows // 8 - 1:
                send(1 - slot, 1, more)

    def step(t, carry):
        def two(j, carry):
            sweep(0, True)
            sweep(1, jnp.logical_or(t < steps - 1, j < SWEEPS // 2 - 1))
            return carry

        lax.fori_loop(0, SWEEPS // 2, two, 0)
        after = lax.rem(t + 1, steps)
        highest[...] = jnp.maximum(highest[...], surface[...])
        source[...] = diag_ref[...] * surface[...] + forcing_ref[after]
        return carry

    lax.fori_loop(0, steps, step, 0)

    for q in range(domains):
        sending[q, :share, :] = highest[q * share : (q + 1) * share, :]
        sending[q, share:, :] = surface[q * share : (q + 1) * share, :]

    def strip(to, by):
        return pltpu.make_async_remote_copy(
            src_ref=sending.at[to],
            dst_ref=landing.at[by],
            send_sem=strip_send.at[to],
            recv_sem=strip_recv.at[by],
            device_id={"dom": to},
            device_id_type=MESH,
        )

    def start(k, carry):
        strip(lax.rem(me + k, domains), me).start()
        return carry

    lax.fori_loop(1, domains, start, 0)
    landing[me] = sending[me]

    def finish(k, carry):
        peer = lax.rem(me + k, domains)
        strip(peer, peer).wait_recv()
        strip(peer, me).wait_send()
        return carry

    lax.fori_loop(1, domains, finish, 0)
    for q in range(domains):
        out_ref[0, q * share : (q + 1) * share, :] = landing[q, :share, :]
        out_ref[1, q * share : (q + 1) * share, :] = landing[q, share:, :]


def grid_kernel(table_ref, nodes_ref, weights_ref, level_ref, final_ref):
    rows, node = table_ref.shape[1:]

    def cells(c, carry):
        at = pl.ds(pl.multiple_of(c * 8, 8), 8)
        totals = [jnp.zeros((8, node), F32)] * 2
        for k in range(nodes_ref.shape[0]):
            index = nodes_ref[k, at, :]
            row, lane = index // node, index % node
            found = [jnp.zeros((8, node), F32)] * 2
            for r in range(rows):
                hit = row == r
                for f in range(2):
                    picked = jnp.take_along_axis(
                        jnp.broadcast_to(table_ref[f, r : r + 1, :], (8, node)), lane, axis=1
                    )
                    found[f] = jnp.where(hit, picked, found[f])
            weight = weights_ref[k, at, :]
            totals = [total + weight * value for total, value in zip(totals, found)]
        level_ref[at, :] = totals[0]
        final_ref[at, :] = totals[1]
        return carry

    lax.fori_loop(0, nodes_ref.shape[1] // 8, cells, 0)


def local(domains, eta_start, forcing, diagonal, coupling, neighbours, wet, grid_nodes, grid_weights):
    steps, rows, node = forcing.shape
    slots = coupling.shape[1]
    share = rows // domains
    vmem = pl.BlockSpec(memory_space=pltpu.VMEM)
    fields = pl.pallas_call(
        functools.partial(surge_kernel, domains),
        out_shape=jax.ShapeDtypeStruct((2, rows, node), F32),
        in_specs=[vmem] * 5 + [pl.BlockSpec(memory_space=pl.ANY)],
        out_specs=vmem,
        scratch_shapes=[
            pltpu.VMEM(coupling.shape, BF16),
            pltpu.VMEM((rows // 2, slots * node, 2 * node), BF16),
            pltpu.VMEM((2, 2 * rows, 2 * node), BF16),
            pltpu.VMEM(((slots - 1) * rows, 2 * rows), BF16),
            pltpu.VMEM((rows, node), F32),
            pltpu.VMEM((rows, node), F32),
            pltpu.VMEM((rows, node), F32),
            pltpu.VMEM((rows, node), F32),
            pltpu.VMEM((rows, node), F32),
            pltpu.VMEM((domains, 2 * share, node), F32),
            pltpu.VMEM((domains, 2 * share, node), F32),
            pltpu.SemaphoreType.DMA((rows // 8,)),
            pltpu.SemaphoreType.DMA((2, 2)),
            pltpu.SemaphoreType.DMA((2, 2)),
            pltpu.SemaphoreType.DMA((domains,)),
            pltpu.SemaphoreType.DMA((domains,)),
        ],
        compiler_params=pltpu.CompilerParams(
            collective_id=0, has_side_effects=True, vmem_limit_bytes=40 << 20
        ),
    )(eta_start, forcing, diagonal, neighbours, wet, coupling)
    cells = grid_nodes.shape[1]
    shaped = (grid_nodes.shape[0], cells // node, node)
    level, final = pl.pallas_call(
        grid_kernel,
        out_shape=[jax.ShapeDtypeStruct((cells // node, node), F32)] * 2,
        in_specs=[vmem] * 3,
        out_specs=[vmem] * 2,
    )(fields, grid_nodes.reshape(shaped), grid_weights.reshape(shaped))
    return level.reshape(-1), final.reshape(-1)


def solution(mesh):
    in_specs = (
        P(("storm", "dom"), None),
        P(None, ("storm", "dom"), None),
        P("dom", None),
        P("dom", None, None, None),
        P("dom", None),
        P("dom", None),
        P(None, "dom"),
        P(None, "dom"),
    )
    out_specs = (P(("storm", "dom")), P(("storm", "dom")))
    return jax.shard_map(
        functools.partial(local, mesh.shape["dom"]),
        mesh=mesh, in_specs=in_specs, out_specs=out_specs, check_vma=False,
    )
```

```python
import functools

import jax
import jax.numpy as jnp
from jax import lax
from jax.experimental import pallas as pl
from jax.experimental.pallas import tpu as pltpu
from jax.sharding import PartitionSpec as P

SWEEPS = 8
MESH = pl.DeviceIdType.MESH
F32, BF16 = jnp.float32, jnp.bfloat16


def surge_kernel(
    domains,
    eta_hbm, forcing_hbm, diag_hbm, nb_hbm, wet_hbm, coupling_ref,
    out_ref,
    eta_ref, forcing_ref, diag_ref, nb_ref, wet_ref, raw, weights, padded, onehot, nearby, surface, source, scale, highest, partial, sending, landing,
    small_sem, load_sem, send_sem, recv_sem, strip_send, strip_recv,
):
    steps, rows, node = forcing_ref.shape
    slots = coupling_ref.shape[1]
    margin = rows // 2
    share = rows // domains
    chunk = 8
    me = lax.axis_index("dom")
    outer = lax.rem(me, 2)
    inner = 1 - outer

    small = [
        pltpu.make_async_copy(source_ref, target_ref, small_sem.at[i])
        for i, (source_ref, target_ref) in enumerate(
            [(eta_hbm, eta_ref), (diag_hbm, diag_ref), (forcing_hbm, forcing_ref), (nb_hbm, nb_ref), (wet_hbm, wet_ref)]
        )
    ]
    for load in small:
        load.start()

    loads = [
        pltpu.make_async_copy(
            coupling_ref.at[pl.ds(c * chunk, chunk)], raw.at[pl.ds(c * chunk, chunk)], load_sem.at[c]
        )
        for c in range(rows // chunk)
    ]
    for load in loads:
        load.start()

    padded[...] = jnp.zeros_like(padded)
    barrier = pltpu.get_barrier_semaphore()

    def greet(k, carry):
        peer = lax.rem(me + k, domains)
        pl.semaphore_signal(barrier, inc=1, device_id={"dom": peer}, device_id_type=MESH)
        return carry

    lax.fori_loop(1, domains, greet, 0)

    for load in small:
        load.wait()
    scale[...] = wet_ref[...].astype(F32) / diag_ref[...]
    lane = lax.broadcasted_iota(jnp.int32, (rows, 2 * rows), 1)
    for s in range(1, slots):
        onehot[(s - 1) * rows : s * rows, :] = (nb_ref[:, s : s + 1] == lane).astype(F32).astype(BF16)

    def split(value):
        high = value.astype(BF16).astype(F32)
        return high, value - high

    def store(slot, row, count):
        high, low = split(surface[pl.ds(row, count), :])
        padded[slot, pl.ds(margin + row, count), :node] = high.astype(BF16)
        padded[slot, pl.ds(margin + row, count), node:] = low.astype(BF16)

    def exchange(slot, side, step):
        return pltpu.make_async_remote_copy(
            src_ref=padded.at[slot, pl.ds(pl.multiple_of(margin + side * margin, margin), margin)],
            dst_ref=padded.at[slot, pl.ds(pl.multiple_of((1 - side) * (margin + rows), margin), margin)],
            send_sem=send_sem.at[slot, side],
            recv_sem=recv_sem.at[slot, side],
            device_id={"dom": me + step * (2 * side - 1)},
            device_id_type=MESH,
        )

    def present(side):
        peer = me + 2 * side - 1
        return jnp.logical_and(peer >= 0, peer < domains)

    def send(slot, side, condition):
        @pl.when(jnp.logical_and(present(side), condition))
        def _():
            exchange(slot, side, 1).start()

    def receive(slot, side):
        @pl.when(present(side))
        def _():
            exchange(slot, 1 - side, -1).wait_recv()
            exchange(slot, side, 1).wait_send()

    surface[...] = eta_ref[...]
    source[...] = diag_ref[...] * eta_ref[...] + forcing_ref[0]
    highest[...] = jnp.full((rows, node), -jnp.inf, F32)
    store(0, 0, rows)

    pl.semaphore_wait(barrier, domains - 1)
    send(0, outer, True)
    send(0, inner, True)

    for c, load in enumerate(loads):
        load.wait()

        def arrange(pair, carry):
            for half in range(2):
                for s in range(slots):
                    weights[pair, s * node : (s + 1) * node, half * node : (half + 1) * node] = raw[
                        2 * pair + half, s
                    ].T
            return carry

        lax.fori_loop(c * chunk // 2, (c + 1) * chunk // 2, arrange, 0)

    sub = lax.broadcasted_iota(jnp.int32, (8, node), 0)

    def products(first_pair, left, first, last):
        result = jnp.zeros((8, node), F32)
        for q in range(4):
            pair = first_pair + q
            both = jnp.dot(
                left, weights[pair, first * node : last * node, :], preferred_element_type=F32
            )
            both = both[:8] + both[8:]
            result = jnp.where(sub == 2 * q, both[:, :node], result)
            result = jnp.where(sub == 2 * q + 1, both[:, node:], result)
        return result

    def sweep(slot, more):
        for group in range(rows // 8):
            at = slice(group * 8, group * 8 + 8)
            left = jnp.concatenate(split(surface[at, :]), axis=0).astype(BF16)
            partial[at, :] = products(group * 4, left, 0, 1)

        receive(slot, inner)
        receive(slot, outer)
        near = jnp.dot(onehot[...], padded[slot], preferred_element_type=F32)
        for s in range(slots - 1):
            nearby[s] = near[s * rows : (s + 1) * rows, :]
        count = rows // 8
        for turn in range(count):
            group = turn + (outer if turn < count // 2 else -outer) * (count // 2)
            at = pl.ds(pl.multiple_of(group * 8, 8), 8)
            left = jnp.concatenate(
                [
                    jnp.concatenate([nearby[s, at, :node], nearby[s, at, node:]], axis=0)
                    for s in range(slots - 1)
                ],
                axis=1,
            ).astype(BF16)
            coupled = partial[at, :] + products(group * 4, left, 1, slots)
            surface[at, :] = (source[at, :] - coupled) * scale[at, :]
            if turn % 2 == 1:
                store(1 - slot, pl.multiple_of(group * 8 - 8, 16), 16)
            if turn == count // 2 - 1:
                send(1 - slot, outer, more)
            if turn == count - 1:
                send(1 - slot, inner, more)

    def step(t, carry):
        def two(j, carry):
            sweep(0, True)
            sweep(1, jnp.logical_or(t < steps - 1, j < SWEEPS // 2 - 1))
            return carry

        lax.fori_loop(0, SWEEPS // 2, two, 0)
        after = lax.rem(t + 1, steps)
        highest[...] = jnp.maximum(highest[...], surface[...])
        source[...] = diag_ref[...] * surface[...] + forcing_ref[after]
        return carry

    lax.fori_loop(0, steps, step, 0)

    for q in range(domains):
        sending[q, :share, :] = highest[q * share : (q + 1) * share, :]
        sending[q, share:, :] = surface[q * share : (q + 1) * share, :]

    def strip(to, by):
        return pltpu.make_async_remote_copy(
            src_ref=sending.at[to],
            dst_ref=landing.at[by],
            send_sem=strip_send.at[to],
            recv_sem=strip_recv.at[by],
            device_id={"dom": to},
            device_id_type=MESH,
        )

    def start(k, carry):
        strip(lax.rem(me + k, domains), me).start()
        return carry

    lax.fori_loop(1, domains, start, 0)
    landing[me] = sending[me]

    def finish(k, carry):
        peer = lax.rem(me + k, domains)
        strip(peer, peer).wait_recv()
        strip(peer, me).wait_send()
        return carry

    lax.fori_loop(1, domains, finish, 0)
    for q in range(domains):
        out_ref[0, q * share : (q + 1) * share, :] = landing[q, :share, :]
        out_ref[1, q * share : (q + 1) * share, :] = landing[q, share:, :]


def grid_kernel(table_ref, nodes_ref, weights_ref, level_ref, final_ref):
    rows, node = table_ref.shape[1:]

    def cells(c, carry):
        at = pl.ds(pl.multiple_of(c * 8, 8), 8)
        span = pl.ds(pl.multiple_of(c * 8 * node, 8 * node), 8 * node)
        totals = [jnp.zeros((8, node), F32)] * 2
        for k in range(nodes_ref.shape[0]):
            index = nodes_ref[k, span].reshape(8, node)
            row, lane = index // node, index % node
            found = [jnp.zeros((8, node), F32)] * 2
            for r in range(rows):
                hit = row == r
                for f in range(2):
                    picked = jnp.take_along_axis(
                        jnp.broadcast_to(table_ref[f, r : r + 1, :], (8, node)), lane, axis=1
                    )
                    found[f] = jnp.where(hit, picked, found[f])
            weight = weights_ref[k, span].reshape(8, node)
            totals = [total + weight * value for total, value in zip(totals, found)]
        level_ref[at, :] = totals[0]
        final_ref[at, :] = totals[1]
        return carry

    lax.fori_loop(0, nodes_ref.shape[1] // (8 * node), cells, 0)


def local(domains, eta_start, forcing, diagonal, coupling, neighbours, wet, grid_nodes, grid_weights):
    steps, rows, node = forcing.shape
    slots = coupling.shape[1]
    share = rows // domains
    vmem = pl.BlockSpec(memory_space=pltpu.VMEM)
    fields = pl.pallas_call(
        functools.partial(surge_kernel, domains),
        out_shape=jax.ShapeDtypeStruct((2, rows, node), F32),
        in_specs=[pl.BlockSpec(memory_space=pl.ANY)] * 6,
        out_specs=vmem,
        scratch_shapes=[
            pltpu.VMEM(eta_start.shape, F32),
            pltpu.VMEM(forcing.shape, F32),
            pltpu.VMEM(diagonal.shape, F32),
            pltpu.VMEM(neighbours.shape, jnp.int32),
            pltpu.VMEM(wet.shape, jnp.int32),
            pltpu.VMEM(coupling.shape, BF16),
            pltpu.VMEM((rows // 2, slots * node, 2 * node), BF16),
            pltpu.VMEM((2, 2 * rows, 2 * node), BF16),
            pltpu.VMEM(((slots - 1) * rows, 2 * rows), BF16),
            pltpu.VMEM((slots - 1, rows, 2 * node), F32),
            pltpu.VMEM((rows, node), F32),
            pltpu.VMEM((rows, node), F32),
            pltpu.VMEM((rows, node), F32),
            pltpu.VMEM((rows, node), F32),
            pltpu.VMEM((rows, node), F32),
            pltpu.VMEM((domains, 2 * share, node), F32),
            pltpu.VMEM((domains, 2 * share, node), F32),
            pltpu.SemaphoreType.DMA((5,)),
            pltpu.SemaphoreType.DMA((rows // 8,)),
            pltpu.SemaphoreType.DMA((2, 2)),
            pltpu.SemaphoreType.DMA((2, 2)),
            pltpu.SemaphoreType.DMA((domains,)),
            pltpu.SemaphoreType.DMA((domains,)),
        ],
        compiler_params=pltpu.CompilerParams(
            collective_id=0, has_side_effects=True, vmem_limit_bytes=56 << 20
        ),
    )(eta_start, forcing, diagonal, neighbours, wet, coupling)
    cells = grid_nodes.shape[1]
    level, final = pl.pallas_call(
        grid_kernel,
        out_shape=[jax.ShapeDtypeStruct((cells // node, node), F32)] * 2,
        in_specs=[vmem] * 3,
        out_specs=[vmem] * 2,
    )(fields, grid_nodes, grid_weights)
    return level.reshape(-1), final.reshape(-1)


def solution(mesh):
    in_specs = (
        P(("storm", "dom"), None),
        P(None, ("storm", "dom"), None),
        P("dom", None),
        P("dom", None, None, None),
        P("dom", None),
        P("dom", None),
        P(None, "dom"),
        P(None, "dom"),
    )
    out_specs = (P(("storm", "dom")), P(("storm", "dom")))
    return jax.shard_map(
        functools.partial(local, mesh.shape["dom"]),
        mesh=mesh, in_specs=in_specs, out_specs=out_specs, check_vma=False,
    )
```

```python
import functools

import jax
import jax.numpy as jnp
from jax import lax
from jax.experimental import pallas as pl
from jax.experimental.pallas import tpu as pltpu
from jax.sharding import PartitionSpec as P

SWEEPS = 8
MESH = pl.DeviceIdType.MESH
F32, BF16 = jnp.float32, jnp.bfloat16


def surge_kernel(
    domains,
    eta_hbm, forcing_hbm, diag_hbm, nb_hbm, wet_hbm, coupling_ref,
    out_ref,
    eta_ref, forcing_ref, diag_ref, nb_ref, wet_ref, raw, weights, padded, onehot, surface, source, scale, highest, partial, sending, landing,
    small_sem, load_sem, send_sem, recv_sem, strip_send, strip_recv,
):
    steps, rows, node = forcing_ref.shape
    slots = coupling_ref.shape[1]
    margin = rows // 2
    share = rows // domains
    chunk = 8
    me = lax.axis_index("dom")
    outer = lax.rem(me, 2)
    inner = 1 - outer

    small = [
        pltpu.make_async_copy(source_ref, target_ref, small_sem.at[i])
        for i, (source_ref, target_ref) in enumerate(
            [(eta_hbm, eta_ref), (diag_hbm, diag_ref), (forcing_hbm, forcing_ref), (nb_hbm, nb_ref), (wet_hbm, wet_ref)]
        )
    ]
    for load in small:
        load.start()

    loads = [
        pltpu.make_async_copy(
            coupling_ref.at[pl.ds(c * chunk, chunk)], raw.at[pl.ds(c * chunk, chunk)], load_sem.at[c]
        )
        for c in range(rows // chunk)
    ]
    for load in loads:
        load.start()

    padded[...] = jnp.zeros_like(padded)
    barrier = pltpu.get_barrier_semaphore()

    def greet(k, carry):
        peer = lax.rem(me + k, domains)
        pl.semaphore_signal(barrier, inc=1, device_id={"dom": peer}, device_id_type=MESH)
        return carry

    lax.fori_loop(1, domains, greet, 0)

    for load in small:
        load.wait()
    scale[...] = wet_ref[...].astype(F32) / diag_ref[...]
    place = lax.broadcasted_iota(jnp.int32, (2 * rows, rows), 0)
    for s in range(1, slots):
        match = (nb_ref[s : s + 1, :] == place).astype(F32)
        match = jnp.concatenate([match, match], axis=1).T.astype(BF16)
        for half in range(2):
            onehot[half, (s - 1) * margin : s * margin, :] = match[half * margin : (half + 1) * margin]

    def split(value):
        high = value.astype(BF16).astype(F32)
        return high, value - high

    def store(slot, row, value):
        at = pl.ds(pl.multiple_of(margin + row, margin), value.shape[0])
        high, low = split(value)
        padded[slot, at, :node] = high.astype(BF16)
        padded[slot, at, node:] = low.astype(BF16)

    def exchange(slot, side, step):
        return pltpu.make_async_remote_copy(
            src_ref=padded.at[slot, pl.ds(pl.multiple_of(margin + side * margin, margin), margin)],
            dst_ref=padded.at[slot, pl.ds(pl.multiple_of((1 - side) * (margin + rows), margin), margin)],
            send_sem=send_sem.at[slot, side],
            recv_sem=recv_sem.at[slot, side],
            device_id={"dom": me + step * (2 * side - 1)},
            device_id_type=MESH,
        )

    def present(side):
        peer = me + 2 * side - 1
        return jnp.logical_and(peer >= 0, peer < domains)

    def send(slot, side, condition):
        @pl.when(jnp.logical_and(present(side), condition))
        def _():
            exchange(slot, side, 1).start()

    def receive(slot, side):
        @pl.when(present(side))
        def _():
            exchange(slot, 1 - side, -1).wait_recv()

    def sent(slot, side, condition):
        @pl.when(jnp.logical_and(present(side), condition))
        def _():
            exchange(slot, side, 1).wait_send()

    surface[...] = eta_ref[...]
    source[...] = diag_ref[...] * eta_ref[...] + forcing_ref[0]
    highest[...] = jnp.full((rows, node), -jnp.inf, F32)
    store(0, 0, eta_ref[...])

    pl.semaphore_wait(barrier, domains - 1)
    send(0, outer, True)
    send(0, inner, True)

    for c, load in enumerate(loads):
        load.wait()

        def arrange(pair, carry):
            for half in range(2):
                for s in range(slots):
                    weights[pair, s * node : (s + 1) * node, half * node : (half + 1) * node] = raw[
                        2 * pair + half, s
                    ].T
            return carry

        lax.fori_loop(c * chunk // 2, (c + 1) * chunk // 2, arrange, 0)

    sub = lax.broadcasted_iota(jnp.int32, (8, node), 0)

    def products(first_pair, left, first, last):
        result = jnp.zeros((8, node), F32)
        for q in range(4):
            pair = first_pair + q
            both = jnp.dot(
                left, weights[pair, first * node : last * node, :], preferred_element_type=F32
            )
            both = both[:8] + both[8:]
            result = jnp.where(sub == 2 * q, both[:, :node], result)
            result = jnp.where(sub == 2 * q + 1, both[:, node:], result)
        return result

    def sweep(slot, later, more):
        sent(1 - slot, inner, later)
        sent(1 - slot, outer, later)
        for group in range(rows // 8):
            at = slice(group * 8, group * 8 + 8)
            left = jnp.concatenate(split(surface[at, :]), axis=0).astype(BF16)
            partial[at, :] = products(group * 4, left, 0, 1)

        receive(slot, inner)
        receive(slot, outer)
        count = margin // 8
        known = padded[slot]
        for half in (outer, inner):
            near = jnp.dot(onehot[half], known, preferred_element_type=F32)
            at = pl.ds(pl.multiple_of(half * margin, margin), margin)
            coupled = []
            for turn in range(count):
                parts = [
                    near[s * margin + turn * 8 : s * margin + turn * 8 + 8] for s in range(slots - 1)
                ]
                left = jnp.concatenate(
                    [jnp.concatenate([part[:, :node], part[:, node:]], axis=0) for part in parts], axis=1
                ).astype(BF16)
                coupled.append(products(half * (margin // 2) + turn * 4, left, 1, slots))
            fresh = (source[at, :] - (partial[at, :] + jnp.concatenate(coupled, axis=0))) * scale[at, :]
            surface[at, :] = fresh
            store(1 - slot, half * margin, fresh)
            send(1 - slot, half, more)

    def step(t, carry):
        def two(j, carry):
            sweep(0, jnp.logical_or(t > 0, j > 0), True)
            sweep(1, True, jnp.logical_or(t < steps - 1, j < SWEEPS // 2 - 1))
            return carry

        lax.fori_loop(0, SWEEPS // 2, two, 0)
        after = lax.rem(t + 1, steps)
        highest[...] = jnp.maximum(highest[...], surface[...])
        source[...] = diag_ref[...] * surface[...] + forcing_ref[after]
        return carry

    lax.fori_loop(0, steps, step, 0)
    sent(1, inner, True)
    sent(1, outer, True)

    for q in range(domains):
        sending[q, :share, :] = highest[q * share : (q + 1) * share, :]
        sending[q, share:, :] = surface[q * share : (q + 1) * share, :]

    def strip(to, by):
        return pltpu.make_async_remote_copy(
            src_ref=sending.at[to],
            dst_ref=landing.at[by],
            send_sem=strip_send.at[to],
            recv_sem=strip_recv.at[by],
            device_id={"dom": to},
            device_id_type=MESH,
        )

    def start(k, carry):
        strip(lax.rem(me + k, domains), me).start()
        return carry

    lax.fori_loop(1, domains, start, 0)
    landing[me] = sending[me]

    def finish(k, carry):
        peer = lax.rem(me + k, domains)
        strip(peer, peer).wait_recv()
        strip(peer, me).wait_send()
        return carry

    lax.fori_loop(1, domains, finish, 0)
    for q in range(domains):
        out_ref[0, q * share : (q + 1) * share, :] = landing[q, :share, :]
        out_ref[1, q * share : (q + 1) * share, :] = landing[q, share:, :]


def grid_kernel(table_ref, nodes_ref, weights_ref, level_ref, final_ref):
    rows, node = table_ref.shape[1:]

    def cells(c, carry):
        at = pl.ds(pl.multiple_of(c * 8, 8), 8)
        span = pl.ds(pl.multiple_of(c * 8 * node, 8 * node), 8 * node)
        totals = [jnp.zeros((8, node), F32)] * 2
        for k in range(nodes_ref.shape[0]):
            index = nodes_ref[k, span].reshape(8, node)
            row, lane = index // node, index % node
            found = [jnp.zeros((8, node), F32)] * 2
            for r in range(rows):
                hit = row == r
                for f in range(2):
                    picked = jnp.take_along_axis(
                        jnp.broadcast_to(table_ref[f, r : r + 1, :], (8, node)), lane, axis=1
                    )
                    found[f] = jnp.where(hit, picked, found[f])
            weight = weights_ref[k, span].reshape(8, node)
            totals = [total + weight * value for total, value in zip(totals, found)]
        level_ref[at, :] = totals[0]
        final_ref[at, :] = totals[1]
        return carry

    lax.fori_loop(0, nodes_ref.shape[1] // (8 * node), cells, 0)


def local(domains, eta_start, forcing, diagonal, coupling, neighbours, wet, grid_nodes, grid_weights):
    steps, rows, node = forcing.shape
    slots = coupling.shape[1]
    share = rows // domains
    vmem = pl.BlockSpec(memory_space=pltpu.VMEM)
    fields = pl.pallas_call(
        functools.partial(surge_kernel, domains),
        out_shape=jax.ShapeDtypeStruct((2, rows, node), F32),
        in_specs=[pl.BlockSpec(memory_space=pl.ANY)] * 6,
        out_specs=vmem,
        scratch_shapes=[
            pltpu.VMEM(eta_start.shape, F32),
            pltpu.VMEM(forcing.shape, F32),
            pltpu.VMEM(diagonal.shape, F32),
            pltpu.VMEM(neighbours.shape[::-1], jnp.int32),
            pltpu.VMEM(wet.shape, jnp.int32),
            pltpu.VMEM(coupling.shape, BF16),
            pltpu.VMEM((rows // 2, slots * node, 2 * node), BF16),
            pltpu.VMEM((2, 2 * rows, 2 * node), BF16),
            pltpu.VMEM((2, (slots - 1) * rows // 2, 2 * rows), BF16),
            pltpu.VMEM((rows, node), F32),
            pltpu.VMEM((rows, node), F32),
            pltpu.VMEM((rows, node), F32),
            pltpu.VMEM((rows, node), F32),
            pltpu.VMEM((rows, node), F32),
            pltpu.VMEM((domains, 2 * share, node), F32),
            pltpu.VMEM((domains, 2 * share, node), F32),
            pltpu.SemaphoreType.DMA((5,)),
            pltpu.SemaphoreType.DMA((rows // 8,)),
            pltpu.SemaphoreType.DMA((2, 2)),
            pltpu.SemaphoreType.DMA((2, 2)),
            pltpu.SemaphoreType.DMA((domains,)),
            pltpu.SemaphoreType.DMA((domains,)),
        ],
        compiler_params=pltpu.CompilerParams(
            collective_id=0, has_side_effects=True, vmem_limit_bytes=56 << 20
        ),
    )(eta_start, forcing, diagonal, neighbours.T, wet, coupling)
    cells = grid_nodes.shape[1]
    level, final = pl.pallas_call(
        grid_kernel,
        out_shape=[jax.ShapeDtypeStruct((cells // node, node), F32)] * 2,
        in_specs=[vmem] * 3,
        out_specs=[vmem] * 2,
    )(fields, grid_nodes, grid_weights)
    return level.reshape(-1), final.reshape(-1)


def solution(mesh):
    in_specs = (
        P(("storm", "dom"), None),
        P(None, ("storm", "dom"), None),
        P("dom", None),
        P("dom", None, None, None),
        P("dom", None),
        P("dom", None),
        P(None, "dom"),
        P(None, "dom"),
    )
    out_specs = (P(("storm", "dom")), P(("storm", "dom")))
    return jax.shard_map(
        functools.partial(local, mesh.shape["dom"]),
        mesh=mesh, in_specs=in_specs, out_specs=out_specs, check_vma=False,
    )
```
